32 devices in a mesh: gx: 8 (over z, x), gy: 4 (over y, core).
Axes of the slice: x: 2, y: 2, z: 4, core: 2. Of those that a mesh axis runs over, the one named last changes fastest.
Arguments:
- surface: float32 [256, 512], P('gx', 'gy'), may hold values from -6 to 6
- velocity_x: float32 [256, 512], P('gx', 'gy'), may hold values from -3 to 3
- velocity_y: float32 [256, 512], P('gx', 'gy'), may hold values from -3 to 3
- classes: int32 [256, 512], P('gx', 'gy'), may hold values from 0 to 7
- wet_mask: int32 [256, 512], P('gx', 'gy'), may hold values 0 or 1
Outputs:
- surface_final: float32 [256, 512], P('gx', 'gy')
- velocity_x_final: float32 [256, 512], P('gx', 'gy')
- velocity_y_final: float32 [256, 512], P('gx', 'gy')
The draws below stay inside these ranges and needn't reach their ends.
All inputs are finite; a program needn't handle non-finite values. No bound on the sum of `wet_mask` on one device may be relied on, other than what follows from the above.
Results may differ from the reference program's by a relative error of at most 0.00002.
Values sent between devices are 32-bit elements; how exact they have to be, the bound alone decides.
No kernel may reach another device: no remote copies, remote signals or barrier semaphores. Data moves between devices by JAX's collectives and lax.ppermute only.
A program may use at most 64 MiB of HBM per device.

```python
import jax
import jax.numpy as jnp

STEPS = 8
NX = 256
NY = 512


def place_ends(entries, own_key, smallest, largest):
    index_at = [jax.random.randint(jax.random.fold_in(own_key, axis), (), 0, length) for axis, length in enumerate(entries.shape)]
    main_axis = entries.shape.index(max(entries.shape))
    neighbour = index_at[:main_axis] + [(index_at[main_axis] + 1) % entries.shape[main_axis]] + index_at[main_axis + 1:]
    return entries.at[tuple(index_at)].set(smallest).at[tuple(neighbour)].set(largest)


def shard_levels(key, shape, cuts, least, largest):
    factor_of = 1.0
    for axis_at, blocks in cuts:
        heights = jax.random.uniform(jax.random.fold_in(jax.random.fold_in(key, 6), axis_at), (blocks,), jnp.float32, least / len(cuts), largest / len(cuts))
        factor_of = factor_of * jnp.repeat(jnp.exp(heights), shape[axis_at] // blocks).reshape((-1,) + (1,) * (len(shape) - 1 - axis_at))
    return factor_of


def bell_draw(stream_key, shape, width, bound, shards=(), dtype=jnp.bfloat16):
    factor_of = shard_levels(stream_key, shape, shards, -0.22, 0.18) if shards else 1.0
    result = jax.random.normal(stream_key, shape, jnp.float32) * width * factor_of
    return jnp.minimum(jnp.maximum(result, -bound), bound).astype(dtype)


def setup_inputs(seed: int = 0) -> dict:
    seeds = jax.random.split(jax.random.key(seed), 6)
    return {
        "surface": bell_draw(seeds[0], (NX, NY), 1.0, 6.0, ((0, 8), (1, 4)), jnp.float32),
        "velocity_x": bell_draw(seeds[1], (NX, NY), 0.5, 3.0, ((0, 8), (1, 4)), jnp.float32),
        "velocity_y": bell_draw(seeds[2], (NX, NY), 0.5, 3.0, ((0, 8), (1, 4)), jnp.float32),
        "classes": place_ends(jax.random.randint(seeds[3], (NX, NY), 0, 8), jax.random.fold_in(seeds[3], 1), 0, 7).astype(jnp.int32),
        "wet_mask": place_ends((jax.random.randint(seeds[4], (NX, NY), 0, 8) < 7).astype(jnp.int32), jax.random.fold_in(seeds[4], 1), 0, 1),
    }


GRAVITY = 1.0
FRICTION = 0.05
TIME_STEP = 1.2


def diff_first(field):
    return (jnp.roll(field, -1, 0) - jnp.roll(field, 1, 0)) * 0.5


def diff_second(field):
    return (jnp.roll(field, -1, 1) - jnp.roll(field, 1, 1)) * 0.5


def laplacian(field):
    return (jnp.roll(field, -1, 0) + jnp.roll(field, 1, 0) + jnp.roll(field, -1, 1) + jnp.roll(field, 1, 1) - 4.0 * field)


def tendency(state, ground_depth, wet):
    elevation, flow_x, flow_y = state
    change_e = -(diff_first(ground_depth * flow_x) + diff_second(ground_depth * flow_y))
    curved = laplacian(elevation)
    coeff = GRAVITY * ground_depth * ground_depth / 3.0
    change_x = wet * (-GRAVITY * diff_first(elevation) - coeff * diff_first(curved) - FRICTION * flow_x)
    change_y = wet * (-GRAVITY * diff_second(elevation) - coeff * diff_second(curved) - FRICTION * flow_y)
    return (change_e, change_x, change_y)


def combine(state, slope, factor):
    return tuple(a + factor * b for a, b in zip(state, slope))


def reference(surface, velocity_x, velocity_y, classes, wet_mask):
    wet = wet_mask.astype(jnp.float32)
    ground_depth = (0.15 + classes.astype(jnp.float32) * (0.4 / 7.0)) * wet
    state = (surface, velocity_x, velocity_y)
    for step_index in range(STEPS):
        first = tendency(state, ground_depth, wet)
        second = tendency(combine(state, first, 0.5 * TIME_STEP), ground_depth, wet)
        third = tendency(combine(state, second, 0.5 * TIME_STEP), ground_depth, wet)
        fourth = tendency(combine(state, third, TIME_STEP), ground_depth, wet)
        state = tuple(s + (TIME_STEP / 6.0) * (a + 2.0 * b + 2.0 * c + d) for s, a, b, c, d in zip(state, first, second, third, fourth))
    return state[0], state[1], state[2]
```

```python
import functools
import math

import jax
import jax.numpy as jnp
from jax import lax
from jax.experimental import pallas as pl
from jax.experimental.pallas import tpu as pltpu
from jax.sharding import PartitionSpec as P

STEPS = 8

GRAVITY = 1.0
FRICTION = 0.05
TIME_STEP = 1.2

HALO = 3 * 2 * STEPS
ROW = 8
FULL = 32
AHEAD = 5
LAG = 8
SEAM = 2
UNROLL = 2
VMEM_LIMIT = 8 * 1024 * 1024

R = FRICTION
POWERS = [
    (1, 0, 0, 0, 0, 0),
    (0, 1, 0, 0, 0, 0),
    (0, -R, 1, 0, 0, 0),
    (0, R**2, -R, 1, 0, 0),
    (0, -(R**3), R**2, -2 * R, 1, 0),
    (0, R**4, -(R**3), 3 * R**2, -2 * R, 1),
]
TAYLOR = [TIME_STEP**n / math.factorial(n) for n in range(5)]
E_NEXT = [sum(TAYLOR[n] * POWERS[n][i] for n in range(5)) for i in range(6)]
G_NEXT = [sum(TAYLOR[n] * POWERS[n + 1][i] for n in range(5)) for i in range(6)]
W_NEXT = [
    sum(TAYLOR[n] * (-R) ** (n - 1 - m) * POWERS[m][i] for n in range(1, 5) for m in range(n))
    for i in range(6)
]
DAMP = sum(TAYLOR[n] * (-R) ** n for n in range(5))

G_SCALE = E_NEXT[1]
K_SCALE = (E_NEXT[2], E_NEXT[4] / E_NEXT[2])
W_SCALE = W_NEXT[0]
KEPT = (1.0, G_SCALE, K_SCALE[0], G_SCALE * K_SCALE[0], K_SCALE[0] * K_SCALE[1], G_SCALE * K_SCALE[0] * K_SCALE[1])
E_MIX = E_NEXT[3] / KEPT[3]
G_MIX = [G_SCALE * weight / kept for weight, kept in zip(G_NEXT, KEPT)]
W_MIX = [weight / (W_SCALE * kept) for weight, kept in zip(W_NEXT, KEPT)]


def move(cells, axis, steps):
    count = lax.axis_size(axis)
    return lax.ppermute(cells, axis, [(i, (i + steps[i % len(steps)]) % count) for i in range(count)])


MOVES = ((2, 2, -1, 1), (-1, 1, 2, 2), (1, -1), (-2,))
OUTER, INNER = (-1, 1), (1, -1)


def is_at(axis, period, *places):
    at = lax.rem(lax.axis_index(axis), period)
    return functools.reduce(jnp.logical_or, [at == place for place in places])


def turned(block, by, axis):
    return pltpu.roll(block, by % block.shape[axis], axis)


def fold(first, second):
    lane = lax.broadcasted_iota(jnp.int32, first.shape, 1)
    return jnp.where(lane < 64, pltpu.roll(first, 96, 1), pltpu.roll(second, 32, 1))


def unfold(both):
    return pltpu.roll(both, 32, 1), pltpu.roll(both, 96, 1)


def gather_kernel(got_4, got_3, got_2, got_1, own, centre, to_outer, to_inner, ends, low, high):
    rest = got_4.shape[1]
    place = [is_at("gx", 4, i) for i in range(4)]
    lower_half = is_at("gx", 4, 0, 1)

    def strip(f):
        one, two, three = got_1[f], got_2[f], got_3[f]
        return jnp.concatenate(
            [
                jnp.where(lower_half, two[-rest:], one[-rest:]),
                jnp.where(place[0], one, jnp.where(place[2], two, three)),
                own[f],
                jnp.where(place[1], one, jnp.where(place[3], two, three)),
                got_4[f],
            ],
            axis=0,
        ).T

    e, p, q, depth = (strip(f) for f in range(4))
    length = q.shape[0]
    row = lax.broadcasted_iota(jnp.int32, q.shape, 0)
    north = jnp.where(row == length - 1, 0.0, turned(q, -1, 0))
    south = jnp.where(row == 0, 0.0, turned(q, 1, 0))
    g = (-0.5 * G_SCALE) * ((turned(p, -1, 1) - turned(p, 1, 1)) + (north - south))
    ends[0:ROW], ends[ROW:] = q[:ROW], q[-ROW:]
    for f, part in enumerate((e, g, depth)):
        centre[f] = part
        at = f * (FULL + ROW)
        low[at:at + FULL] = part[:FULL]
        low[at + FULL:at + FULL + ROW] = fold(part[FULL:FULL + ROW], part[FULL + ROW:HALO])
        high[at:at + ROW] = fold(part[-HALO:ROW - HALO], part[ROW - HALO:-FULL])
        high[at + ROW:at + ROW + FULL] = part[-FULL:]
    at = 3 * (FULL + ROW)
    low[at:], high[at:] = q[:ROW], q[-ROW:]
    first_y = is_at("gy", 2, 0)
    to_inner[...] = jnp.where(first_y, high[...], low[...])
    to_outer[...] = jnp.where(first_y, low[...], high[...])


def weighted(weights, values):
    total = None
    for weight, value in zip(weights, values):
        if weight:
            term = value if weight == 1 else weight * value
            total = term if total is None else total + term
    return total


class Rows:
    def __init__(self, blocks, source):
        self.blocks, self.source = blocks, source

    def __getitem__(self, k):
        return self.source[k]

    def __setitem__(self, k, value):
        self.source[k] = value

    def north(self, k):
        return self[k + 1] if k < self.blocks - 1 else turned(self[0], -1, 0)

    def south(self, k):
        return self[k - 1] if k > 0 else turned(self[self.blocks - 1], 1, 0)


class Slope:
    def __init__(self, blocks, ref, alpha, beta, alpha_east, beta_east, diverge=True):
        self.field = Rows(blocks, ref)
        self.alpha, self.beta, self.alpha_east, self.beta_east = alpha, beta, alpha_east, beta_east
        self.diverge = diverge
        self.east_2, self.along, self.sums_east, self.wait, self.x_west = {}, {}, {}, {}, {}
        self.dy, self.lift = {}, {}
        self.sums, self.y = Rows(blocks, {}), Rows(blocks, {})

    def rotate(self, k):
        self.east_2[k] = turned(self.field[k], -2, 1)

    def rotate_sum(self, k):
        here, east_2 = self.field[k], self.east_2.pop(k)
        self.along[k] = turned(east_2 + here, 1, 1)
        self.wait[k] = self.alpha_east[k] * (east_2 - here)

    def sum_up(self, k):
        north, south = self.field.north(k), self.field.south(k)
        self.dy[k] = north - south
        total = self.along.pop(k) + (north + south)
        self.sums[k] = total
        self.sums_east[k] = turned(total, -2, 1)

    def slope_y(self, k):
        s = self.sums
        self.y[k] = self.alpha[k] * self.dy.pop(k) + self.beta[k] * (s.north(k) - s.south(k))

    def lift_y(self, k):
        if self.diverge:
            self.lift[k] = self.y.north(k) - self.y.south(k)

    def slope_x(self, k):
        x = self.wait.pop(k) + self.beta_east[k] * (self.sums_east.pop(k) - self.sums[k])
        self.x_west[k] = turned(x, 2 if self.diverge else 1, 1)
        if self.diverge:
            self.wait[k] = x + self.lift.pop(k)

    def divergence(self, k):
        return self.wait.pop(k) - self.x_west.pop(k)


class Memo:
    def __init__(self, make):
        self.make, self.made = make, {}

    def __getitem__(self, k):
        if k not in self.made:
            self.made[k] = self.make(k)
        return self.made[k]


def parts_of(blocks):
    top = 2 * AHEAD
    assert top + 2 * LAG <= blocks - 2 and 4 + 2 * SEAM <= LAG
    return (
        ("finish", top + 2 * LAG, 2),
        ("sum_up", top, 0),
        ("slope_y", top + 2, 1),
        ("lift_y", top + 4, 2),
        ("slope_x", top + LAG, 2),
        ("rotate_sum", AHEAD, 0),
        ("rotate", 0, 0),
    )


def emit(blocks, sweeps):
    edge = {
        "slope_y": {0: 1, blocks - 1: 1},
        "lift_y": {0: 2, blocks - 1: 2, 1: 1, blocks - 2: 1},
    }
    parts = parts_of(blocks)
    slots = {}
    for number, (slopes, finish) in enumerate(sweeps):
        for order, (name, begin, ahead) in enumerate(parts):
            for i in range(blocks):
                k = (i + ahead + 3 * number) % blocks
                slot = number * blocks + begin + i + SEAM * edge.get(name, {}).get(k, 0)
                slots.setdefault(slot, []).append((number, order, name, k))
    for slot in sorted(slots):
        for number, _, name, k in sorted(slots[slot]):
            slopes, finish = sweeps[number]
            if name == "finish":
                finish(k)
            else:
                for slope in slopes:
                    getattr(slope, name)(k)


def step_kernel(outer, inner, centre, ends, own, flow_x, flow_y, out_e, out_x, out_y,
                rows, low, high, e, g, e1, g1, total_e, *coefficients):
    length = centre.shape[1]
    total = length + 2 * HALO
    blocks = total // ROW
    first_y = is_at("gy", 2, 0)
    low[...] = jnp.where(first_y, outer[...], inner[...])
    high[...] = jnp.where(first_y, inner[...], outer[...])
    for f in range(3):
        at = f * (FULL + ROW)
        rows[f, 0:ROW], rows[f, ROW:2 * ROW] = unfold(low[at:at + ROW])
        rows[f, 2 * ROW:HALO] = low[at + ROW:at + ROW + FULL]
        rows[f, HALO:HALO + length] = centre[f]
        rows[f, HALO + length:HALO + length + FULL] = high[at:at + FULL]
        rows[f, total - 2 * ROW:total - ROW], rows[f, total - ROW:total] = unfold(high[at + FULL:at + FULL + ROW])
    last = 3 * (FULL + ROW)
    for at, given in (
        (HALO, low[last + ROW - 1:last + ROW]),
        (HALO + length - 1, -high[last:last + 1]),
        (HALO - 1, -ends[0:1]),
        (HALO + length, ends[2 * ROW - 1:2 * ROW]),
    ):
        rows[1, at:at + 1] = rows[1, at:at + 1] + (0.5 * G_SCALE) * given

    def strided(k):
        return pl.ds(k, ROW, stride=blocks)

    for k in range(blocks):
        e[k] = rows[0, strided(k), :]
        g[k] = rows[1, strided(k), :]
        total_e[k] = jnp.zeros((ROW, e.shape[2]), jnp.float32)
        depth = rows[2, strided(k), :]
        cube = depth * depth * depth * (GRAVITY / 12.0)
        slow = 0.25 * GRAVITY * depth - 4.0 * cube
        both = (slow, cube, turned(slow, -1, 1), turned(cube, -1, 1))
        for n in range(2):
            for ref, value in zip(coefficients[4 * n:4 * n + 4], both):
                ref[k] = K_SCALE[n] * value

    def slopes_of(n, *refs):
        return tuple(Slope(blocks, ref, *coefficients[4 * n:4 * n + 4]) for ref in refs)

    def one_step():
        first, second = slopes_of(0, e, g), slopes_of(1, e1, g1)

        def finish(k):
            e1[k], g1[k] = first[0].divergence(k), first[1].divergence(k)

        def finish_step(k):
            parts = (e[k], g[k], e1[k], g1[k], second[0].divergence(k), second[1].divergence(k))
            total_e[k] = DAMP * total_e[k] + parts[0] + weighted(W_MIX[1:4], parts[1:4])
            e[k] = (parts[0] + parts[1]) + (parts[2] + parts[4]) + E_MIX * parts[3]
            g[k] = weighted(G_MIX, parts)

        return [(first, finish), (second, finish_step)]

    def some_steps(_, carry):
        emit(blocks, [sweep for _ in range(UNROLL) for sweep in one_step()])
        return carry

    lax.fori_loop(0, STEPS // UNROLL, some_steps, 0)

    def square(k):
        depth = rows[2, strided(k), :]
        return depth * depth * (GRAVITY / 3.0 * W_SCALE)

    a = Memo(lambda k: -0.5 * GRAVITY * W_SCALE + 2.0 * square(k))
    b = Memo(lambda k: -0.5 * square(k))
    a_east, b_east = Memo(lambda k: turned(a[k], -1, 1)), Memo(lambda k: turned(b[k], -1, 1))
    slope = Slope(blocks, total_e, a, b, a_east, b_east, diverge=False)

    def finish_velocity(k):
        rows[0, strided(k), :] = e[k]
        rows[1, strided(k), :] = slope.x_west[k]
        rows[2, strided(k), :] = slope.y[k]

    emit(blocks, [((slope,), finish_velocity)])

    def tile(f):
        return rows[f, HALO:HALO + length].T[HALO:HALO + out_e.shape[0]]

    wet = own[3] > 0.0
    out_e[...] = tile(0)
    for out, flow, f in ((out_x, flow_x, 1), (out_y, flow_y, 2)):
        before = flow[...]
        out[...] = jnp.where(wet, DAMP**STEPS * before + tile(f), before)


def on_device(surface, velocity_x, velocity_y, classes, wet_mask):
    width, length = surface.shape
    wet = wet_mask.astype(jnp.float32)
    depth = (0.15 + classes.astype(jnp.float32) * (0.4 / 7.0)) * wet
    own = jnp.stack([surface, depth * velocity_x, depth * velocity_y, depth])
    rest = HALO - width
    got_1, got_2, got_3 = (move(own, "gx", steps) for steps in MOVES[:3])
    got_4 = move(own[:, :rest], "gx", MOVES[3])
    lanes = width + 2 * HALO
    f32 = jnp.float32
    packet = jax.ShapeDtypeStruct((3 * (FULL + ROW) + ROW, lanes), f32)
    centre, to_outer, to_inner, ends = pl.pallas_call(
        gather_kernel,
        out_shape=(
            jax.ShapeDtypeStruct((3, length, lanes), f32),
            packet,
            packet,
            jax.ShapeDtypeStruct((2 * ROW, lanes), f32),
        ),
        scratch_shapes=[pltpu.VMEM(packet.shape, f32)] * 2,
        compiler_params=pltpu.CompilerParams(vmem_limit_bytes=VMEM_LIMIT),
        name="turn",
    )(got_4, got_3, got_2, got_1, own)
    inner = move(to_inner, "gy", INNER)
    outer = move(to_outer, "gy", OUTER)
    total = length + 2 * HALO
    blocked = pltpu.VMEM((total // ROW, ROW, lanes), f32)
    return pl.pallas_call(
        step_kernel,
        out_shape=tuple(jax.ShapeDtypeStruct((width, length), f32) for _ in range(3)),
        scratch_shapes=[pltpu.VMEM((3, total, lanes), f32)] + [pltpu.VMEM(packet.shape, f32)] * 2 + [blocked] * 13,
        compiler_params=pltpu.CompilerParams(vmem_limit_bytes=VMEM_LIMIT),
        name="steps",
    )(outer, inner, centre, ends, own, velocity_x, velocity_y)


def solution(mesh):
    return jax.shard_map(
        on_device,
        mesh=mesh,
        in_specs=(P("gx", "gy"),) * 5,
        out_specs=(P("gx", "gy"),) * 3,
        check_vma=False,
    )
```

```python
import functools
import math

import jax
import jax.numpy as jnp
from jax import lax
from jax.experimental import pallas as pl
from jax.experimental.pallas import tpu as pltpu
from jax.sharding import PartitionSpec as P

STEPS = 8

GRAVITY = 1.0
FRICTION = 0.05
TIME_STEP = 1.2

HALO = 3 * 2 * STEPS
ROW = 8
FULL = 32
MOVE = 6
LAST = 2
UNROLL = 1
VMEM_LIMIT = 8 * 1024 * 1024

R = FRICTION
POWERS = [
    (1, 0, 0, 0, 0, 0),
    (0, 1, 0, 0, 0, 0),
    (0, -R, 1, 0, 0, 0),
    (0, R**2, -R, 1, 0, 0),
    (0, -(R**3), R**2, -2 * R, 1, 0),
    (0, R**4, -(R**3), 3 * R**2, -2 * R, 1),
]
TAYLOR = [TIME_STEP**n / math.factorial(n) for n in range(5)]
E_NEXT = [sum(TAYLOR[n] * POWERS[n][i] for n in range(5)) for i in range(6)]
G_NEXT = [sum(TAYLOR[n] * POWERS[n + 1][i] for n in range(5)) for i in range(6)]
W_NEXT = [
    sum(TAYLOR[n] * (-R) ** (n - 1 - m) * POWERS[m][i] for n in range(1, 5) for m in range(n))
    for i in range(6)
]
DAMP = sum(TAYLOR[n] * (-R) ** n for n in range(5))

G_SCALE = E_NEXT[1]
K_SCALE = (E_NEXT[2], E_NEXT[4] / E_NEXT[2])
W_SCALE = W_NEXT[0]
KEPT = (1.0, G_SCALE, K_SCALE[0], G_SCALE * K_SCALE[0], K_SCALE[0] * K_SCALE[1], G_SCALE * K_SCALE[0] * K_SCALE[1])
E_MIX = E_NEXT[3] / KEPT[3]
G_MIX = [G_SCALE * weight / kept for weight, kept in zip(G_NEXT, KEPT)]
W_MIX = [weight / (W_SCALE * kept) for weight, kept in zip(W_NEXT, KEPT)]


def move(cells, axis, steps):
    count = lax.axis_size(axis)
    return lax.ppermute(cells, axis, [(i, (i + steps[i % len(steps)]) % count) for i in range(count)])


MOVES = ((2, 2, -1, 1), (-1, 1, 2, 2), (1, -1), (-2,))
OUTER, INNER = (-1, 1), (1, -1)


def is_at(axis, period, *places):
    at = lax.rem(lax.axis_index(axis), period)
    return functools.reduce(jnp.logical_or, [at == place for place in places])


def turned(block, by, axis):
    return pltpu.roll(block, by % block.shape[axis], axis)


def fold(first, second):
    lane = lax.broadcasted_iota(jnp.int32, first.shape, 1)
    return jnp.where(lane < 64, pltpu.roll(first, 96, 1), pltpu.roll(second, 32, 1))


def unfold(both):
    return pltpu.roll(both, 32, 1), pltpu.roll(both, 96, 1)


def gather_kernel(got_4, got_3, got_2, got_1, own, centre, to_outer, to_inner, ends, low, high):
    rest = got_4.shape[1]
    place = [is_at("gx", 4, i) for i in range(4)]
    lower_half = is_at("gx", 4, 0, 1)

    def strip(f):
        one, two, three = got_1[f], got_2[f], got_3[f]
        return jnp.concatenate(
            [
                jnp.where(lower_half, two[-rest:], one[-rest:]),
                jnp.where(place[0], one, jnp.where(place[2], two, three)),
                own[f],
                jnp.where(place[1], one, jnp.where(place[3], two, three)),
                got_4[f],
            ],
            axis=0,
        ).T

    e, p, q, depth = (strip(f) for f in range(4))
    length = q.shape[0]
    row = lax.broadcasted_iota(jnp.int32, q.shape, 0)
    north = jnp.where(row == length - 1, 0.0, turned(q, -1, 0))
    south = jnp.where(row == 0, 0.0, turned(q, 1, 0))
    g = (-0.5 * G_SCALE) * ((turned(p, -1, 1) - turned(p, 1, 1)) + (north - south))
    ends[0:ROW], ends[ROW:] = q[:ROW], q[-ROW:]
    for f, part in enumerate((e, g, depth)):
        centre[f] = part
        at = f * (FULL + ROW)
        low[at:at + FULL] = part[:FULL]
        low[at + FULL:at + FULL + ROW] = fold(part[FULL:FULL + ROW], part[FULL + ROW:HALO])
        high[at:at + ROW] = fold(part[-HALO:ROW - HALO], part[ROW - HALO:-FULL])
        high[at + ROW:at + ROW + FULL] = part[-FULL:]
    at = 3 * (FULL + ROW)
    low[at:], high[at:] = q[:ROW], q[-ROW:]
    first_y = is_at("gy", 2, 0)
    to_inner[...] = jnp.where(first_y, high[...], low[...])
    to_outer[...] = jnp.where(first_y, low[...], high[...])


def weighted(weights, values):
    total = None
    for weight, value in zip(weights, values):
        if weight:
            term = value if weight == 1 else weight * value
            total = term if total is None else total + term
    return total


class Rows:
    def __init__(self, blocks, source):
        self.blocks, self.source, self.seam = blocks, source, {}

    def __getitem__(self, k):
        return self.source[k]

    def __setitem__(self, k, value):
        self.source[k] = value

    def over_seam(self, k):
        if k not in self.seam:
            self.seam[k] = turned(self[k], -1 if k == 0 else 1, 0)
        return self.seam[k]

    def north(self, k):
        return self[k + 1] if k < self.blocks - 1 else self.over_seam(0)

    def south(self, k):
        return self[k - 1] if k > 0 else self.over_seam(self.blocks - 1)


class Slope:
    AHEAD, LAG, SEAM = 5, 8, 2
    EDGE = ("slope_y",)

    @classmethod
    def parts(cls):
        top = 2 * cls.AHEAD
        assert 4 + 2 * cls.SEAM <= cls.LAG
        return (
            ("finish", top + 2 * cls.LAG, 2),
            ("sum_up", top, 0),
            ("slope_y", top + 2, 1),
            ("lift_y", top + 4, 2),
            ("slope_x", top + cls.LAG, 2),
            ("rotate_sum", cls.AHEAD, 0),
            ("rotate", 0, 0),
        )

    def __init__(self, blocks, ref, alpha, beta, alpha_east, beta_east, diverge=True):
        self.field = Rows(blocks, ref)
        self.alpha, self.beta, self.alpha_east, self.beta_east = alpha, beta, alpha_east, beta_east
        self.diverge = diverge
        self.east_2, self.along, self.sums_east, self.wait, self.x_west = {}, {}, {}, {}, {}
        self.dy, self.lift = {}, {}
        self.sums, self.y = Rows(blocks, {}), Rows(blocks, {})

    def rotate(self, k):
        self.east_2[k] = turned(self.field[k], -2, 1)

    def rotate_sum(self, k):
        here, east_2 = self.field[k], self.east_2.pop(k)
        self.along[k] = turned(east_2 + here, 1, 1)
        self.wait[k] = self.alpha_east[k] * (east_2 - here)

    def sum_up(self, k):
        north, south = self.field.north(k), self.field.south(k)
        self.dy[k] = north - south
        total = self.along.pop(k) + (north + south)
        self.sums[k] = total
        self.sums_east[k] = turned(total, -2, 1)

    def slope_y(self, k):
        s = self.sums
        self.y[k] = self.alpha[k] * self.dy.pop(k) + self.beta[k] * (s.north(k) - s.south(k))

    def lift_y(self, k):
        if self.diverge:
            self.lift[k] = self.y.north(k) - self.y.south(k)

    def slope_x(self, k):
        x = self.wait.pop(k) + self.beta_east[k] * (self.sums_east.pop(k) - self.sums[k])
        self.x_west[k] = turned(x, 2 if self.diverge else 1, 1)
        if self.diverge:
            self.wait[k] = x + self.lift.pop(k)

    def divergence(self, k):
        return self.wait.pop(k) - self.x_west.pop(k)


class QuickSlope:
    AHEAD, LAG, SEAM = 6, 6, 2
    EDGE = ("slope_x", "slope_y")

    @classmethod
    def parts(cls):
        assert 1 + 2 * cls.SEAM <= cls.LAG
        return (
            ("finish", cls.AHEAD + 3 + cls.LAG, 2),
            ("sum_up", cls.AHEAD, 0),
            ("slope_x", cls.AHEAD + 2, 1),
            ("slope_y", cls.AHEAD + 2, 1),
            ("lift_y", cls.AHEAD + 4, 2),
            ("rotate", 0, 0),
        )

    def __init__(self, blocks, ref, alpha, beta, alpha_east, beta_east, diverge=True):
        self.blocks, self.diverge = blocks, diverge
        self.alpha, self.beta, self.alpha_east, self.beta_east = alpha, beta, alpha_east, beta_east
        self.field = Rows(blocks, ref)
        self.at, self.far, self.dx, self.dy, self.x, self.x_west = {}, {}, {}, {}, {}, {}
        self.east_2, self.sums, self.y = (Rows(blocks, {}) for _ in range(3))

    def rotate(self, k):
        here = self.field[k]
        self.at[k] = tuple(turned(here, by, 1) for by in (-1, 1, -3))
        self.east_2[k] = turned(here, -2, 1)
        if k in (0, self.blocks - 1):
            self.field.over_seam(k)

    def sum_up(self, k):
        east_1, west_1, east_3 = self.at.pop(k)
        north, south = self.field.north(k), self.field.south(k)
        self.dy[k] = north - south
        self.sums[k] = (east_1 + west_1) + (north + south)
        self.far[k] = east_3 + east_1
        self.dx[k] = self.east_2[k] - self.field[k]
        if k in (0, self.blocks - 1):
            self.sums.over_seam(k)
            self.east_2.over_seam(k)

    def slope_x(self, k):
        sums_east = self.far.pop(k) + (self.east_2.north(k) + self.east_2.south(k))
        x = self.alpha_east[k] * self.dx.pop(k) + self.beta_east[k] * (sums_east - self.sums[k])
        self.x[k] = x
        self.x_west[k] = turned(x, 2 if self.diverge else 1, 1)

    def slope_y(self, k):
        s = self.sums
        self.y[k] = self.alpha[k] * self.dy.pop(k) + self.beta[k] * (s.north(k) - s.south(k))
        if k in (0, self.blocks - 1):
            self.y.over_seam(k)

    def lift_y(self, k):
        if self.diverge:
            self.x[k] = self.x[k] + (self.y.north(k) - self.y.south(k))

    def divergence(self, k):
        return self.x.pop(k) - self.x_west.pop(k)


class Memo:
    def __init__(self, make):
        self.make, self.made = make, {}

    def __getitem__(self, k):
        if k not in self.made:
            self.made[k] = self.make(k)
        return self.made[k]


def emit(blocks, sweeps):
    kind = type(sweeps[0][0][0])
    seam = kind.SEAM
    edge = {name: {0: seam, blocks - 1: seam} for name in kind.EDGE}
    edge["lift_y"] = {0: 2 * seam, blocks - 1: 2 * seam, 1: seam, blocks - 2: seam}
    parts = kind.parts()
    every = max(blocks, parts[0][1] + 1)
    slots = {}
    for number in range(len(sweeps)):
        for order, (name, begin, ahead) in enumerate(parts):
            for i in range(blocks):
                k = (i + ahead + 3 * number) % blocks
                slot = number * every + begin + i + edge.get(name, {}).get(k, 0)
                slots.setdefault(slot, []).append((number, order, name, k))
    for slot in sorted(slots):
        for number, _, name, k in sorted(slots[slot]):
            slopes, finish = sweeps[number]
            if name == "finish":
                finish(k)
            else:
                for slope in slopes:
                    getattr(slope, name)(k)


def step_kernel(outer, inner, centre, ends, own, flow_x, flow_y, out_e, out_x, out_y,
                rows, low, high, kept, e, g, e1, g1, total_e, *coefficients):
    length = centre.shape[1]
    total = length + 2 * HALO
    blocks = total // ROW
    first_y = is_at("gy", 2, 0)
    low[...] = jnp.where(first_y, outer[...], inner[...])
    high[...] = jnp.where(first_y, inner[...], outer[...])
    for f in range(3):
        at = f * (FULL + ROW)
        rows[f, 0:ROW], rows[f, ROW:2 * ROW] = unfold(low[at:at + ROW])
        rows[f, 2 * ROW:HALO] = low[at + ROW:at + ROW + FULL]
        rows[f, HALO:HALO + length] = centre[f]
        rows[f, HALO + length:HALO + length + FULL] = high[at:at + FULL]
        rows[f, total - 2 * ROW:total - ROW], rows[f, total - ROW:total] = unfold(high[at + FULL:at + FULL + ROW])
    last = 3 * (FULL + ROW)
    for at, given in (
        (HALO, low[last + ROW - 1:last + ROW]),
        (HALO + length - 1, -high[last:last + 1]),
        (HALO - 1, -ends[0:1]),
        (HALO + length, ends[2 * ROW - 1:2 * ROW]),
    ):
        rows[1, at:at + 1] = rows[1, at:at + 1] + (0.5 * G_SCALE) * given

    def strided(k):
        return pl.ds(k, ROW, stride=blocks)

    def set_coefficients(k, depth):
        cube = depth * depth * depth * (GRAVITY / 12.0)
        slow = 0.25 * GRAVITY * depth - 4.0 * cube
        both = (slow, cube, turned(slow, -1, 1), turned(cube, -1, 1))
        for n in range(2):
            for ref, value in zip(coefficients[4 * n:4 * n + 4], both):
                ref[k] = K_SCALE[n] * value

    for k in range(blocks):
        e[k] = rows[0, strided(k), :]
        g[k] = rows[1, strided(k), :]
        total_e[k] = jnp.zeros((ROW, e.shape[2]), jnp.float32)
        set_coefficients(k, rows[2, strided(k), :])

    def one_step(kind, count):
        first, second = (
            tuple(kind(count, ref, *coefficients[4 * n:4 * n + 4]) for ref in refs)
            for n, refs in enumerate(((e, g), (e1, g1)))
        )

        def finish(k):
            e1[k], g1[k] = first[0].divergence(k), first[1].divergence(k)

        def finish_step(k):
            parts = (e[k], g[k], e1[k], g1[k], second[0].divergence(k), second[1].divergence(k))
            total_e[k] = DAMP * total_e[k] + parts[0] + weighted(W_MIX[1:4], parts[1:4])
            e[k] = (parts[0] + parts[1]) + (parts[2] + parts[4]) + E_MIX * parts[3]
            g[k] = weighted(G_MIX, parts)

        return [(first, finish), (second, finish_step)]

    def some_steps(_, carry):
        emit(blocks, [sweep for _ in range(UNROLL) for sweep in one_step(Slope, blocks)])
        return carry

    lax.fori_loop(0, (STEPS - LAST) // UNROLL, some_steps, 0)

    margin, half = MOVE * LAST, length // 2
    few = (half + 2 * margin) // ROW
    for f, ref in ((0, e), (1, g), (3, total_e)):
        for k in range(blocks):
            rows[f, strided(k), :] = ref[k]

    def folded(f, k):
        first, second = (
            rows[f, pl.ds(HALO - margin + start + k, ROW, stride=few), :] for start in (0, half)
        )
        return fold(first, second)

    for k in range(few):
        e[k], g[k], total_e[k], kept[k] = (folded(f, k) for f in (0, 1, 3, 2))
        set_coefficients(k, kept[k])

    def last_step(_, carry):
        emit(few, one_step(QuickSlope, few))
        return carry

    lax.fori_loop(0, LAST, last_step, 0)

    square = Memo(lambda k: kept[k] * kept[k] * (GRAVITY / 3.0 * W_SCALE))
    a = Memo(lambda k: -0.5 * GRAVITY * W_SCALE + 2.0 * square[k])
    b = Memo(lambda k: -0.5 * square[k])
    a_east, b_east = Memo(lambda k: turned(a[k], -1, 1)), Memo(lambda k: turned(b[k], -1, 1))
    slope = QuickSlope(few, total_e, a, b, a_east, b_east, diverge=False)

    def finish_velocity(k):
        at = pl.ds(k, ROW, stride=few)
        rows[0, at, :] = e[k]
        rows[1, at, :] = slope.x_west[k]
        rows[2, at, :] = slope.y[k]

    emit(few, [((slope,), finish_velocity)])

    def tile(f):
        width = out_e.shape[0]
        both = rows[f, margin:margin + length].T
        first = HALO - 32
        low_rows, high_rows = both[first:first + width], both[64 + first:64 + first + width]
        lane = lax.broadcasted_iota(jnp.int32, low_rows.shape, 1)
        return jnp.where(lane < half, low_rows, pltpu.roll(high_rows, half, 1))

    wet = own[3] > 0.0
    out_e[...] = tile(0)
    for out, flow, f in ((out_x, flow_x, 1), (out_y, flow_y, 2)):
        before = flow[...]
        out[...] = jnp.where(wet, DAMP**STEPS * before + tile(f), before)


def on_device(surface, velocity_x, velocity_y, classes, wet_mask):
    width, length = surface.shape
    wet = wet_mask.astype(jnp.float32)
    depth = (0.15 + classes.astype(jnp.float32) * (0.4 / 7.0)) * wet
    own = jnp.stack([surface, depth * velocity_x, depth * velocity_y, depth])
    rest = HALO - width
    got_1, got_2, got_3 = (move(own, "gx", steps) for steps in MOVES[:3])
    got_4 = move(own[:, :rest], "gx", MOVES[3])
    lanes = width + 2 * HALO
    f32 = jnp.float32
    packet = jax.ShapeDtypeStruct((3 * (FULL + ROW) + ROW, lanes), f32)
    centre, to_outer, to_inner, ends = pl.pallas_call(
        gather_kernel,
        out_shape=(
            jax.ShapeDtypeStruct((3, length, lanes), f32),
            packet,
            packet,
            jax.ShapeDtypeStruct((2 * ROW, lanes), f32),
        ),
        scratch_shapes=[pltpu.VMEM(packet.shape, f32)] * 2,
        compiler_params=pltpu.CompilerParams(vmem_limit_bytes=VMEM_LIMIT),
        name="turn",
    )(got_4, got_3, got_2, got_1, own)
    inner = move(to_inner, "gy", INNER)
    outer = move(to_outer, "gy", OUTER)
    total = length + 2 * HALO
    blocked = pltpu.VMEM((total // ROW, ROW, lanes), f32)
    return pl.pallas_call(
        step_kernel,
        out_shape=tuple(jax.ShapeDtypeStruct((width, length), f32) for _ in range(3)),
        scratch_shapes=[pltpu.VMEM((4, total, lanes), f32)] + [pltpu.VMEM(packet.shape, f32)] * 2 + [blocked] * 14,
        compiler_params=pltpu.CompilerParams(vmem_limit_bytes=VMEM_LIMIT),
        name="steps",
    )(outer, inner, centre, ends, own, velocity_x, velocity_y)


def solution(mesh):
    return jax.shard_map(
        on_device,
        mesh=mesh,
        in_specs=(P("gx", "gy"),) * 5,
        out_specs=(P("gx", "gy"),) * 3,
        check_vma=False,
    )
```

```python
import functools
import math

import jax
import jax.numpy as jnp
from jax import lax
from jax.experimental import pallas as pl
from jax.experimental.pallas import tpu as pltpu
from jax.sharding import PartitionSpec as P

STEPS = 8

GRAVITY = 1.0
FRICTION = 0.05
TIME_STEP = 1.2

HALO = 3 * 2 * STEPS
ROW = 8
FULL = 32
MOVE = 6
LAST = 2
UNROLL = 3
VMEM_LIMIT = 8 * 1024 * 1024

R = FRICTION
POWERS = [
    (1, 0, 0, 0, 0, 0),
    (0, 1, 0, 0, 0, 0),
    (0, -R, 1, 0, 0, 0),
    (0, R**2, -R, 1, 0, 0),
    (0, -(R**3), R**2, -2 * R, 1, 0),
    (0, R**4, -(R**3), 3 * R**2, -2 * R, 1),
]
TAYLOR = [TIME_STEP**n / math.factorial(n) for n in range(5)]
E_NEXT = [sum(TAYLOR[n] * POWERS[n][i] for n in range(5)) for i in range(6)]
G_NEXT = [sum(TAYLOR[n] * POWERS[n + 1][i] for n in range(5)) for i in range(6)]
W_NEXT = [
    sum(TAYLOR[n] * (-R) ** (n - 1 - m) * POWERS[m][i] for n in range(1, 5) for m in range(n))
    for i in range(6)
]
DAMP = sum(TAYLOR[n] * (-R) ** n for n in range(5))

G_SCALE = E_NEXT[1]
K_SCALE = (E_NEXT[2], E_NEXT[4] / E_NEXT[2])
W_SCALE = W_NEXT[0]
KEPT = (1.0, G_SCALE, K_SCALE[0], G_SCALE * K_SCALE[0], K_SCALE[0] * K_SCALE[1], G_SCALE * K_SCALE[0] * K_SCALE[1])
E_MIX = E_NEXT[3] / KEPT[3]
G_MIX = [G_SCALE * weight / kept for weight, kept in zip(G_NEXT, KEPT)]
W_MIX = [weight / (W_SCALE * kept) for weight, kept in zip(W_NEXT, KEPT)]


def move(cells, axis, steps):
    count = lax.axis_size(axis)
    return lax.ppermute(cells, axis, [(i, (i + steps[i % len(steps)]) % count) for i in range(count)])


MOVES = ((2, 2, -1, 1), (-1, 1, 2, 2), (1, -1), (-2,))
OUTER, INNER = (-1, 1), (1, -1)


def is_at(axis, period, *places):
    at = lax.rem(lax.axis_index(axis), period)
    return functools.reduce(jnp.logical_or, [at == place for place in places])


def turned(block, by, axis):
    return pltpu.roll(block, by % block.shape[axis], axis)


def fold(first, second):
    lane = lax.broadcasted_iota(jnp.int32, first.shape, 1)
    return jnp.where(lane < 64, pltpu.roll(first, 96, 1), pltpu.roll(second, 32, 1))


def unfold(both):
    return pltpu.roll(both, 32, 1), pltpu.roll(both, 96, 1)


def gather_kernel(got_4, got_3, got_2, got_1, own, centre, to_outer, to_inner, ends, low, high):
    rest = got_4.shape[1]
    place = [is_at("gx", 4, i) for i in range(4)]
    lower_half = is_at("gx", 4, 0, 1)

    def strip(f):
        one, two, three = got_1[f], got_2[f], got_3[f]
        return jnp.concatenate(
            [
                jnp.where(lower_half, two[-rest:], one[-rest:]),
                jnp.where(place[0], one, jnp.where(place[2], two, three)),
                own[f],
                jnp.where(place[1], one, jnp.where(place[3], two, three)),
                got_4[f],
            ],
            axis=0,
        ).T

    e, p, q, depth = (strip(f) for f in range(4))
    length = q.shape[0]
    row = lax.broadcasted_iota(jnp.int32, q.shape, 0)
    north = jnp.where(row == length - 1, 0.0, turned(q, -1, 0))
    south = jnp.where(row == 0, 0.0, turned(q, 1, 0))
    g = (-0.5 * G_SCALE) * ((turned(p, -1, 1) - turned(p, 1, 1)) + (north - south))
    ends[0:ROW], ends[ROW:] = q[:ROW], q[-ROW:]
    for f, part in enumerate((e, g, depth)):
        centre[f] = part
        at = f * (FULL + ROW)
        low[at:at + FULL] = part[:FULL]
        low[at + FULL:at + FULL + ROW] = fold(part[FULL:FULL + ROW], part[FULL + ROW:HALO])
        high[at:at + ROW] = fold(part[-HALO:ROW - HALO], part[ROW - HALO:-FULL])
        high[at + ROW:at + ROW + FULL] = part[-FULL:]
    at = 3 * (FULL + ROW)
    low[at:], high[at:] = q[:ROW], q[-ROW:]
    first_y = is_at("gy", 2, 0)
    to_inner[...] = jnp.where(first_y, high[...], low[...])
    to_outer[...] = jnp.where(first_y, low[...], high[...])


def weighted(weights, values):
    total = None
    for weight, value in zip(weights, values):
        if weight:
            term = value if weight == 1 else weight * value
            total = term if total is None else total + term
    return total


class Rows:
    def __init__(self, blocks, source):
        self.blocks, self.source, self.seam = blocks, source, {}

    def __getitem__(self, k):
        return self.source[k]

    def __setitem__(self, k, value):
        self.source[k] = value

    def over_seam(self, k):
        if k not in self.seam:
            self.seam[k] = turned(self[k], -1 if k == 0 else 1, 0)
        return self.seam[k]

    def north(self, k):
        return self[k + 1] if k < self.blocks - 1 else self.over_seam(0)

    def south(self, k):
        return self[k - 1] if k > 0 else self.over_seam(self.blocks - 1)


class Slope:
    AHEAD, LAG, SEAM = 5, 8, 2
    EDGE = ("slope_y",)

    @classmethod
    def parts(cls):
        top = 2 * cls.AHEAD
        assert 4 + 2 * cls.SEAM <= cls.LAG
        return (
            ("finish", top + 2 * cls.LAG, 2),
            ("sum_up", top, 0),
            ("slope_y", top + 2, 1),
            ("lift_y", top + 4, 2),
            ("slope_x", top + cls.LAG, 2),
            ("rotate_sum", cls.AHEAD, 0),
            ("rotate", 0, 0),
        )

    def __init__(self, blocks, ref, alpha, beta, alpha_east, beta_east, diverge=True):
        self.field = Rows(blocks, ref)
        self.alpha, self.beta, self.alpha_east, self.beta_east = alpha, beta, alpha_east, beta_east
        self.diverge = diverge
        self.east_2, self.along, self.sums_east, self.wait, self.x_west = {}, {}, {}, {}, {}
        self.dy, self.lift = {}, {}
        self.sums, self.y = Rows(blocks, {}), Rows(blocks, {})

    def rotate(self, k):
        self.east_2[k] = turned(self.field[k], -2, 1)

    def rotate_sum(self, k):
        here, east_2 = self.field[k], self.east_2.pop(k)
        self.along[k] = turned(east_2 + here, 1, 1)
        self.wait[k] = self.alpha_east[k] * (east_2 - here)

    def sum_up(self, k):
        north, south = self.field.north(k), self.field.south(k)
        self.dy[k] = north - south
        total = self.along.pop(k) + (north + south)
        self.sums[k] = total
        self.sums_east[k] = turned(total, -2, 1)

    def slope_y(self, k):
        s = self.sums
        self.y[k] = self.alpha[k] * self.dy.pop(k) + self.beta[k] * (s.north(k) - s.south(k))

    def lift_y(self, k):
        if self.diverge:
            self.lift[k] = self.y.north(k) - self.y.south(k)

    def slope_x(self, k):
        x = self.wait.pop(k) + self.beta_east[k] * (self.sums_east.pop(k) - self.sums[k])
        self.x_west[k] = turned(x, 2 if self.diverge else 1, 1)
        if self.diverge:
            self.wait[k] = x + self.lift.pop(k)

    def divergence(self, k):
        return self.wait.pop(k) - self.x_west.pop(k)


class QuickSlope:
    AHEAD, LAG, SEAM = 6, 6, 2
    EDGE = ("slope_x", "slope_y")

    @classmethod
    def parts(cls):
        assert 1 + 2 * cls.SEAM <= cls.LAG
        return (
            ("finish", cls.AHEAD + 3 + cls.LAG, 2),
            ("sum_up", cls.AHEAD, 0),
            ("slope_x", cls.AHEAD + 2, 1),
            ("slope_y", cls.AHEAD + 2, 1),
            ("lift_y", cls.AHEAD + 4, 2),
            ("rotate", 0, 0),
        )

    def __init__(self, blocks, ref, alpha, beta, alpha_east, beta_east, diverge=True):
        self.blocks, self.diverge = blocks, diverge
        self.alpha, self.beta, self.alpha_east, self.beta_east = alpha, beta, alpha_east, beta_east
        self.field = Rows(blocks, ref)
        self.at, self.far, self.dx, self.dy, self.x, self.x_west = {}, {}, {}, {}, {}, {}
        self.east_2, self.sums, self.y = (Rows(blocks, {}) for _ in range(3))

    def rotate(self, k):
        here = self.field[k]
        self.at[k] = tuple(turned(here, by, 1) for by in (-1, 1, -3))
        self.east_2[k] = turned(here, -2, 1)
        if k in (0, self.blocks - 1):
            self.field.over_seam(k)

    def sum_up(self, k):
        east_1, west_1, east_3 = self.at.pop(k)
        north, south = self.field.north(k), self.field.south(k)
        self.dy[k] = north - south
        self.sums[k] = (east_1 + west_1) + (north + south)
        self.far[k] = east_3 + east_1
        self.dx[k] = self.east_2[k] - self.field[k]
        if k in (0, self.blocks - 1):
            self.sums.over_seam(k)
            self.east_2.over_seam(k)

    def slope_x(self, k):
        sums_east = self.far.pop(k) + (self.east_2.north(k) + self.east_2.south(k))
        x = self.alpha_east[k] * self.dx.pop(k) + self.beta_east[k] * (sums_east - self.sums[k])
        self.x[k] = x
        self.x_west[k] = turned(x, 2 if self.diverge else 1, 1)

    def slope_y(self, k):
        s = self.sums
        self.y[k] = self.alpha[k] * self.dy.pop(k) + self.beta[k] * (s.north(k) - s.south(k))
        if k in (0, self.blocks - 1):
            self.y.over_seam(k)

    def lift_y(self, k):
        if self.diverge:
            self.x[k] = self.x[k] + (self.y.north(k) - self.y.south(k))

    def divergence(self, k):
        return self.x.pop(k) - self.x_west.pop(k)


class Memo:
    def __init__(self, make):
        self.make, self.made = make, {}

    def __getitem__(self, k):
        if k not in self.made:
            self.made[k] = self.make(k)
        return self.made[k]


def emit(blocks, sweeps):
    kind = type(sweeps[0][0][0])
    seam = kind.SEAM
    edge = {name: {0: seam, blocks - 1: seam} for name in kind.EDGE}
    edge["lift_y"] = {0: 2 * seam, blocks - 1: 2 * seam, 1: seam, blocks - 2: seam}
    parts = kind.parts()
    every = max(blocks, parts[0][1] + 1)
    slots = {}
    for number in range(len(sweeps)):
        for order, (name, begin, ahead) in enumerate(parts):
            for i in range(blocks):
                k = (i + ahead + 3 * number) % blocks
                slot = number * every + begin + i + edge.get(name, {}).get(k, 0)
                slots.setdefault(slot, []).append((number, order, name, k))
    for slot in sorted(slots):
        for number, _, name, k in sorted(slots[slot]):
            slopes, finish = sweeps[number]
            if name == "finish":
                finish(k)
            else:
                for slope in slopes:
                    getattr(slope, name)(k)


def step_kernel(outer, inner, centre, ends, own, flow_x, flow_y, out_e, out_x, out_y,
                rows, low, high, kept, e, g, e1, g1, total_e, *coefficients):
    length = centre.shape[1]
    total = length + 2 * HALO
    blocks = total // ROW
    first_y = is_at("gy", 2, 0)
    low[...] = jnp.where(first_y, outer[...], inner[...])
    high[...] = jnp.where(first_y, inner[...], outer[...])
    for f in range(3):
        at = f * (FULL + ROW)
        rows[f, 0:ROW], rows[f, ROW:2 * ROW] = unfold(low[at:at + ROW])
        rows[f, 2 * ROW:HALO] = low[at + ROW:at + ROW + FULL]
        rows[f, HALO:HALO + length] = centre[f]
        rows[f, HALO + length:HALO + length + FULL] = high[at:at + FULL]
        rows[f, total - 2 * ROW:total - ROW], rows[f, total - ROW:total] = unfold(high[at + FULL:at + FULL + ROW])
    last = 3 * (FULL + ROW)
    for at, given in (
        (HALO, low[last + ROW - 1:last + ROW]),
        (HALO + length - 1, -high[last:last + 1]),
        (HALO - 1, -ends[0:1]),
        (HALO + length, ends[2 * ROW - 1:2 * ROW]),
    ):
        rows[1, at:at + 1] = rows[1, at:at + 1] + (0.5 * G_SCALE) * given

    def strided(k):
        return pl.ds(k, ROW, stride=blocks)

    def set_coefficients(k, depth):
        cube = depth * depth * depth * (GRAVITY / 12.0)
        slow = 0.25 * GRAVITY * depth - 4.0 * cube
        both = (slow, cube, turned(slow, -1, 1), turned(cube, -1, 1))
        for n in range(2):
            for ref, value in zip(coefficients[4 * n:4 * n + 4], both):
                ref[k] = K_SCALE[n] * value

    for k in range(blocks):
        e[k] = rows[0, strided(k), :]
        g[k] = rows[1, strided(k), :]
        total_e[k] = jnp.zeros((ROW, e.shape[2]), jnp.float32)
        set_coefficients(k, rows[2, strided(k), :])

    def one_step(kind, count):
        first, second = (
            tuple(kind(count, ref, *coefficients[4 * n:4 * n + 4]) for ref in refs)
            for n, refs in enumerate(((e, g), (e1, g1)))
        )

        def finish(k):
            e1[k], g1[k] = first[0].divergence(k), first[1].divergence(k)

        def finish_step(k):
            parts = (e[k], g[k], e1[k], g1[k], second[0].divergence(k), second[1].divergence(k))
            total_e[k] = DAMP * total_e[k] + parts[0] + weighted(W_MIX[1:4], parts[1:4])
            e[k] = (parts[0] + parts[1]) + (parts[2] + parts[4]) + E_MIX * parts[3]
            g[k] = weighted(G_MIX, parts)

        return [(first, finish), (second, finish_step)]

    def some_steps(_, carry):
        emit(blocks, [sweep for _ in range(UNROLL) for sweep in one_step(Slope, blocks)])
        return carry

    lax.fori_loop(0, (STEPS - LAST) // UNROLL, some_steps, 0)

    margin, half = MOVE * LAST, length // 2
    few = (half + 2 * margin) // ROW
    for f, ref in ((0, e), (1, g), (3, total_e)):
        for k in range(blocks):
            rows[f, strided(k), :] = ref[k]

    def folded(f, k):
        first, second = (
            rows[f, pl.ds(HALO - margin + start + k, ROW, stride=few), :] for start in (0, half)
        )
        return fold(first, second)

    for k in range(few):
        e[k], g[k], total_e[k], kept[k] = (folded(f, k) for f in (0, 1, 3, 2))
        set_coefficients(k, kept[k])

    def last_step(_, carry):
        emit(few, one_step(QuickSlope, few))
        return carry

    lax.fori_loop(0, LAST, last_step, 0)

    square = Memo(lambda k: kept[k] * kept[k] * (GRAVITY / 3.0 * W_SCALE))
    a = Memo(lambda k: -0.5 * GRAVITY * W_SCALE + 2.0 * square[k])
    b = Memo(lambda k: -0.5 * square[k])
    a_east, b_east = Memo(lambda k: turned(a[k], -1, 1)), Memo(lambda k: turned(b[k], -1, 1))
    slope = QuickSlope(few, total_e, a, b, a_east, b_east, diverge=False)

    def finish_velocity(k):
        at = pl.ds(k, ROW, stride=few)
        rows[0, at, :] = e[k]
        rows[1, at, :] = slope.x_west[k]
        rows[2, at, :] = slope.y[k]

    emit(few, [((slope,), finish_velocity)])

    def tile(f):
        width = out_e.shape[0]
        both = rows[f, margin:margin + length].T
        first = HALO - 32
        low_rows, high_rows = both[first:first + width], both[64 + first:64 + first + width]
        lane = lax.broadcasted_iota(jnp.int32, low_rows.shape, 1)
        return jnp.where(lane < half, low_rows, pltpu.roll(high_rows, half, 1))

    wet = own[3] > 0.0
    out_e[...] = tile(0)
    for out, flow, f in ((out_x, flow_x, 1), (out_y, flow_y, 2)):
        before = flow[...]
        out[...] = jnp.where(wet, DAMP**STEPS * before + tile(f), before)


def on_device(surface, velocity_x, velocity_y, classes, wet_mask):
    width, length = surface.shape
    wet = wet_mask.astype(jnp.float32)
    depth = (0.15 + classes.astype(jnp.float32) * (0.4 / 7.0)) * wet
    own = jnp.stack([surface, depth * velocity_x, depth * velocity_y, depth])
    rest = HALO - width
    got_1, got_2, got_3 = (move(own, "gx", steps) for steps in MOVES[:3])
    got_4 = move(own[:, :rest], "gx", MOVES[3])
    lanes = width + 2 * HALO
    f32 = jnp.float32
    packet = jax.ShapeDtypeStruct((3 * (FULL + ROW) + ROW, lanes), f32)
    centre, to_outer, to_inner, ends = pl.pallas_call(
        gather_kernel,
        out_shape=(
            jax.ShapeDtypeStruct((3, length, lanes), f32),
            packet,
            packet,
            jax.ShapeDtypeStruct((2 * ROW, lanes), f32),
        ),
        scratch_shapes=[pltpu.VMEM(packet.shape, f32)] * 2,
        compiler_params=pltpu.CompilerParams(vmem_limit_bytes=VMEM_LIMIT),
        name="turn",
    )(got_4, got_3, got_2, got_1, own)
    inner = move(to_inner, "gy", INNER)
    outer = move(to_outer, "gy", OUTER)
    total = length + 2 * HALO
    blocked = pltpu.VMEM((total // ROW, ROW, lanes), f32)
    return pl.pallas_call(
        step_kernel,
        out_shape=tuple(jax.ShapeDtypeStruct((width, length), f32) for _ in range(3)),
        scratch_shapes=[pltpu.VMEM((4, total, lanes), f32)] + [pltpu.VMEM(packet.shape, f32)] * 2 + [blocked] * 14,
        compiler_params=pltpu.CompilerParams(vmem_limit_bytes=VMEM_LIMIT),
        name="steps",
    )(outer, inner, centre, ends, own, velocity_x, velocity_y)


def solution(mesh):
    return jax.shard_map(
        on_device,
        mesh=mesh,
        in_specs=(P("gx", "gy"),) * 5,
        out_specs=(P("gx", "gy"),) * 3,
        check_vma=False,
    )
```

```python
import functools
import math

import jax
import jax.numpy as jnp
from jax import lax
from jax.experimental import pallas as pl
from jax.experimental.pallas import tpu as pltpu
from jax.sharding import PartitionSpec as P

STEPS = 8

GRAVITY = 1.0
FRICTION = 0.05
TIME_STEP = 1.2

HALO = 3 * 2 * STEPS
ROW = 8
FULL = 32
MOVE = 6
LAST = 2
VMEM_LIMIT = 8 * 1024 * 1024

R = FRICTION
POWERS = [
    (1, 0, 0, 0, 0, 0),
    (0, 1, 0, 0, 0, 0),
    (0, -R, 1, 0, 0, 0),
    (0, R**2, -R, 1, 0, 0),
    (0, -(R**3), R**2, -2 * R, 1, 0),
    (0, R**4, -(R**3), 3 * R**2, -2 * R, 1),
]
TAYLOR = [TIME_STEP**n / math.factorial(n) for n in range(5)]
E_NEXT = [sum(TAYLOR[n] * POWERS[n][i] for n in range(5)) for i in range(6)]
G_NEXT = [sum(TAYLOR[n] * POWERS[n + 1][i] for n in range(5)) for i in range(6)]
W_NEXT = [
    sum(TAYLOR[n] * (-R) ** (n - 1 - m) * POWERS[m][i] for n in range(1, 5) for m in range(n))
    for i in range(6)
]
DAMP = sum(TAYLOR[n] * (-R) ** n for n in range(5))

G_SCALE = E_NEXT[1]
K_SCALE = (E_NEXT[2], E_NEXT[4] / E_NEXT[2])
W_SCALE = W_NEXT[0]
KEPT = (1.0, G_SCALE, K_SCALE[0], G_SCALE * K_SCALE[0], K_SCALE[0] * K_SCALE[1], G_SCALE * K_SCALE[0] * K_SCALE[1])
E_MIX = E_NEXT[3] / KEPT[3]
G_MIX = [G_SCALE * weight / kept for weight, kept in zip(G_NEXT, KEPT)]
W_MIX = [weight / (W_SCALE * kept) for weight, kept in zip(W_NEXT, KEPT)]


def move(cells, axis, steps):
    count = lax.axis_size(axis)
    return lax.ppermute(cells, axis, [(i, (i + steps[i % len(steps)]) % count) for i in range(count)])


MOVES = ((2, 2, -1, 1), (-1, 1, 2, 2), (1, -1), (-2,))
OUTER, INNER = (-1, 1), (1, -1)


def is_at(axis, period, *places):
    at = lax.rem(lax.axis_index(axis), period)
    return functools.reduce(jnp.logical_or, [at == place for place in places])


def turned(block, by, axis):
    return pltpu.roll(block, by % block.shape[axis], axis)


def fold(first, second):
    lane = lax.broadcasted_iota(jnp.int32, first.shape, 1)
    return jnp.where(lane < 64, pltpu.roll(first, 96, 1), pltpu.roll(second, 32, 1))


def unfold(both):
    return pltpu.roll(both, 32, 1), pltpu.roll(both, 96, 1)


def gather_kernel(got_4, got_3, got_2, got_1, own, centre, to_outer, to_inner, ends, low, high):
    rest = got_4.shape[1]
    place = [is_at("gx", 4, i) for i in range(4)]
    lower_half = is_at("gx", 4, 0, 1)

    def strip(f):
        one, two, three = got_1[f], got_2[f], got_3[f]
        return jnp.concatenate(
            [
                jnp.where(lower_half, two[-rest:], one[-rest:]),
                jnp.where(place[0], one, jnp.where(place[2], two, three)),
                own[f],
                jnp.where(place[1], one, jnp.where(place[3], two, three)),
                got_4[f],
            ],
            axis=0,
        ).T

    e, p, q, depth = (strip(f) for f in range(4))
    length = q.shape[0]
    row = lax.broadcasted_iota(jnp.int32, q.shape, 0)
    north = jnp.where(row == length - 1, 0.0, turned(q, -1, 0))
    south = jnp.where(row == 0, 0.0, turned(q, 1, 0))
    g = (-0.5 * G_SCALE) * ((turned(p, -1, 1) - turned(p, 1, 1)) + (north - south))
    ends[0:ROW], ends[ROW:] = q[:ROW], q[-ROW:]
    for f, part in enumerate((e, g, depth)):
        centre[f] = part
        at = f * (FULL + ROW)
        low[at:at + FULL] = part[:FULL]
        low[at + FULL:at + FULL + ROW] = fold(part[FULL:FULL + ROW], part[FULL + ROW:HALO])
        high[at:at + ROW] = fold(part[-HALO:ROW - HALO], part[ROW - HALO:-FULL])
        high[at + ROW:at + ROW + FULL] = part[-FULL:]
    at = 3 * (FULL + ROW)
    low[at:], high[at:] = q[:ROW], q[-ROW:]
    first_y = is_at("gy", 2, 0)
    to_inner[...] = jnp.where(first_y, high[...], low[...])
    to_outer[...] = jnp.where(first_y, low[...], high[...])


def weighted(weights, values):
    total = None
    for weight, value in zip(weights, values):
        if weight:
            term = value if weight == 1 else weight * value
            total = term if total is None else total + term
    return total


class Rows:
    def __init__(self, blocks, source):
        self.blocks, self.source, self.seam = blocks, source, {}

    def __getitem__(self, k):
        return self.source[k]

    def __setitem__(self, k, value):
        self.source[k] = value

    def over_seam(self, k):
        if k not in self.seam:
            self.seam[k] = turned(self[k], -1 if k == 0 else 1, 0)
        return self.seam[k]

    def north(self, k):
        return self[k + 1] if k < self.blocks - 1 else self.over_seam(0)

    def south(self, k):
        return self[k - 1] if k > 0 else self.over_seam(self.blocks - 1)


class Slope:
    AHEAD, LAG, SEAM = 5, 8, 2
    EDGE = ("slope_y",)

    @classmethod
    def parts(cls):
        top = 2 * cls.AHEAD
        assert 4 + 2 * cls.SEAM <= cls.LAG
        return (
            ("finish", top + 2 * cls.LAG, 2),
            ("sum_up", top, 0),
            ("slope_y", top + 2, 1),
            ("lift_y", top + 4, 2),
            ("slope_x", top + cls.LAG, 2),
            ("rotate_sum", cls.AHEAD, 0),
            ("rotate", 0, 0),
        )

    def __init__(self, blocks, ref, alpha, beta, alpha_east, beta_east, diverge=True):
        self.field = Rows(blocks, ref)
        self.alpha, self.beta, self.alpha_east, self.beta_east = alpha, beta, alpha_east, beta_east
        self.diverge = diverge
        self.east_2, self.along, self.sums_east, self.wait, self.x_west = {}, {}, {}, {}, {}
        self.dy, self.lift = {}, {}
        self.sums, self.y = Rows(blocks, {}), Rows(blocks, {})

    def rotate(self, k):
        self.east_2[k] = turned(self.field[k], -2, 1)

    def rotate_sum(self, k):
        here, east_2 = self.field[k], self.east_2.pop(k)
        self.along[k] = turned(east_2 + here, 1, 1)
        self.wait[k] = self.alpha_east[k] * (east_2 - here)

    def sum_up(self, k):
        north, south = self.field.north(k), self.field.south(k)
        self.dy[k] = north - south
        total = self.along.pop(k) + (north + south)
        self.sums[k] = total
        self.sums_east[k] = turned(total, -2, 1)

    def slope_y(self, k):
        s = self.sums
        self.y[k] = self.alpha[k] * self.dy.pop(k) + self.beta[k] * (s.north(k) - s.south(k))

    def lift_y(self, k):
        if self.diverge:
            self.lift[k] = self.y.north(k) - self.y.south(k)

    def slope_x(self, k):
        x = self.wait.pop(k) + self.beta_east[k] * (self.sums_east.pop(k) - self.sums[k])
        self.x_west[k] = turned(x, 2 if self.diverge else 1, 1)
        if self.diverge:
            self.wait[k] = x + self.lift.pop(k)

    def divergence(self, k):
        return self.wait.pop(k) - self.x_west.pop(k)


class QuickSlope:
    AHEAD, LAG, SEAM = 6, 6, 2
    EDGE = ("slope_x", "slope_y")

    @classmethod
    def parts(cls):
        assert 1 + 2 * cls.SEAM <= cls.LAG
        return (
            ("finish", cls.AHEAD + 3 + cls.LAG, 2),
            ("sum_up", cls.AHEAD, 0),
            ("slope_x", cls.AHEAD + 2, 1),
            ("slope_y", cls.AHEAD + 2, 1),
            ("lift_y", cls.AHEAD + 4, 2),
            ("rotate", 0, 0),
        )

    def __init__(self, blocks, ref, alpha, beta, alpha_east, beta_east, diverge=True):
        self.blocks, self.diverge = blocks, diverge
        self.alpha, self.beta, self.alpha_east, self.beta_east = alpha, beta, alpha_east, beta_east
        self.field = Rows(blocks, ref)
        self.at, self.far, self.dx, self.dy, self.x, self.x_west = {}, {}, {}, {}, {}, {}
        self.east_2, self.sums, self.y = (Rows(blocks, {}) for _ in range(3))

    def rotate(self, k):
        here = self.field[k]
        self.at[k] = tuple(turned(here, by, 1) for by in (-1, 1, -3))
        self.east_2[k] = turned(here, -2, 1)
        if k in (0, self.blocks - 1):
            self.field.over_seam(k)

    def sum_up(self, k):
        east_1, west_1, east_3 = self.at.pop(k)
        north, south = self.field.north(k), self.field.south(k)
        self.dy[k] = north - south
        self.sums[k] = (east_1 + west_1) + (north + south)
        self.far[k] = east_3 + east_1
        self.dx[k] = self.east_2[k] - self.field[k]
        if k in (0, self.blocks - 1):
            self.sums.over_seam(k)
            self.east_2.over_seam(k)

    def slope_x(self, k):
        sums_east = self.far.pop(k) + (self.east_2.north(k) + self.east_2.south(k))
        x = self.alpha_east[k] * self.dx.pop(k) + self.beta_east[k] * (sums_east - self.sums[k])
        self.x[k] = x
        self.x_west[k] = turned(x, 2 if self.diverge else 1, 1)

    def slope_y(self, k):
        s = self.sums
        self.y[k] = self.alpha[k] * self.dy.pop(k) + self.beta[k] * (s.north(k) - s.south(k))
        if k in (0, self.blocks - 1):
            self.y.over_seam(k)

    def lift_y(self, k):
        if self.diverge:
            self.x[k] = self.x[k] + (self.y.north(k) - self.y.south(k))

    def divergence(self, k):
        return self.x.pop(k) - self.x_west.pop(k)


class Memo:
    def __init__(self, make):
        self.make, self.made = make, {}

    def __getitem__(self, k):
        if k not in self.made:
            self.made[k] = self.make(k)
        return self.made[k]


def emit(blocks, sweeps):
    kind = type(sweeps[0][0][0])
    seam = kind.SEAM
    edge = {name: {0: seam, blocks - 1: seam} for name in kind.EDGE}
    edge["lift_y"] = {0: 2 * seam, blocks - 1: 2 * seam, 1: seam, blocks - 2: seam}
    parts = kind.parts()
    every = max(blocks, parts[0][1] + 1)
    slots = {}
    for number in range(len(sweeps)):
        for order, (name, begin, ahead) in enumerate(parts):
            for i in range(blocks):
                k = (i + ahead + 3 * number) % blocks
                slot = number * every + begin + i + edge.get(name, {}).get(k, 0)
                slots.setdefault(slot, []).append((number, order, name, k))
    for slot in sorted(slots):
        for number, _, name, k in sorted(slots[slot]):
            slopes, finish = sweeps[number]
            if name == "finish":
                finish(k)
            else:
                for slope in slopes:
                    getattr(slope, name)(k)


def step_kernel(outer, inner, centre, ends, own, flow_x, flow_y, out_e, out_x, out_y,
                rows, low, high, kept, e, g, e1, g1, total_e, *coefficients):
    length = centre.shape[1]
    total = length + 2 * HALO
    blocks = total // ROW
    first_y = is_at("gy", 2, 0)
    low[...] = jnp.where(first_y, outer[...], inner[...])
    high[...] = jnp.where(first_y, inner[...], outer[...])
    for f in range(3):
        at = f * (FULL + ROW)
        rows[f, 0:ROW], rows[f, ROW:2 * ROW] = unfold(low[at:at + ROW])
        rows[f, 2 * ROW:HALO] = low[at + ROW:at + ROW + FULL]
        rows[f, HALO:HALO + length] = centre[f]
        rows[f, HALO + length:HALO + length + FULL] = high[at:at + FULL]
        rows[f, total - 2 * ROW:total - ROW], rows[f, total - ROW:total] = unfold(high[at + FULL:at + FULL + ROW])
    last = 3 * (FULL + ROW)
    for at, given in (
        (HALO, low[last + ROW - 1:last + ROW]),
        (HALO + length - 1, -high[last:last + 1]),
        (HALO - 1, -ends[0:1]),
        (HALO + length, ends[2 * ROW - 1:2 * ROW]),
    ):
        rows[1, at:at + 1] = rows[1, at:at + 1] + (0.5 * G_SCALE) * given

    def strided(k):
        return pl.ds(k, ROW, stride=blocks)

    def set_coefficients(k, depth):
        cube = depth * depth * depth * (GRAVITY / 12.0)
        slow = 0.25 * GRAVITY * depth - 4.0 * cube
        both = (slow, cube, turned(slow, -1, 1), turned(cube, -1, 1))
        for n in range(2):
            for ref, value in zip(coefficients[4 * n:4 * n + 4], both):
                ref[k] = K_SCALE[n] * value

    for k in range(blocks):
        e[k] = rows[0, strided(k), :]
        g[k] = rows[1, strided(k), :]
        set_coefficients(k, rows[2, strided(k), :])

    def weigh_in(k, parts, is_first):
        now = parts[0] + weighted(W_MIX[1:4], parts[1:4])
        total_e[k] = now if is_first else DAMP * total_e[k] + now

    def one_step(kind, count, is_first=False):
        first, second = (
            tuple(kind(count, ref, *coefficients[4 * n:4 * n + 4]) for ref in refs)
            for n, refs in enumerate(((e, g), (e1, g1)))
        )

        def finish(k):
            e1[k], g1[k] = first[0].divergence(k), first[1].divergence(k)

        def finish_step(k):
            parts = (e[k], g[k], e1[k], g1[k], second[0].divergence(k), second[1].divergence(k))
            weigh_in(k, parts, is_first)
            e[k] = (parts[0] + parts[1]) + (parts[2] + parts[4]) + E_MIX * parts[3]
            g[k] = weighted(G_MIX, parts)

        return [(first, finish), (second, finish_step)]

    emit(blocks, [sweep for n in range(STEPS - LAST) for sweep in one_step(Slope, blocks, n == 0)])

    margin, half = MOVE * LAST, length // 2
    few = (half + 2 * margin) // ROW
    for f, ref in ((0, e), (1, g), (3, total_e)):
        for k in range(blocks):
            rows[f, strided(k), :] = ref[k]

    def folded(f, k):
        first, second = (
            rows[f, pl.ds(HALO - margin + start + k, ROW, stride=few), :] for start in (0, half)
        )
        return fold(first, second)

    for k in range(few):
        e[k], g[k], total_e[k], kept[k] = (folded(f, k) for f in (0, 1, 3, 2))
        set_coefficients(k, kept[k])

    square = Memo(lambda k: kept[k] * kept[k] * (GRAVITY / 3.0 * W_SCALE))
    a = Memo(lambda k: -0.5 * GRAVITY * W_SCALE + 2.0 * square[k])
    b = Memo(lambda k: -0.5 * square[k])
    a_east, b_east = Memo(lambda k: turned(a[k], -1, 1)), Memo(lambda k: turned(b[k], -1, 1))
    first = tuple(QuickSlope(few, ref, *coefficients[:4]) for ref in (e, g))
    second = QuickSlope(few, e1, *coefficients[4:])
    slope = QuickSlope(few, total_e, a, b, a_east, b_east, diverge=False)

    def finish_first(k):
        e1[k], g1[k] = first[0].divergence(k), first[1].divergence(k)
        weigh_in(k, (e[k], g[k], e1[k], g1[k]), False)

    def finish_last(k):
        at = pl.ds(k, ROW, stride=few)
        rows[0, at, :] = (e[k] + g[k]) + (e1[k] + second.divergence(k)) + E_MIX * g1[k]
        rows[1, at, :] = slope.x_west[k]
        rows[2, at, :] = slope.y[k]

    before_last = [sweep for _ in range(LAST - 1) for sweep in one_step(QuickSlope, few)]
    emit(few, before_last + [(first, finish_first), ((second, slope), finish_last)])

    def tile(f):
        width = out_e.shape[0]
        both = rows[f, margin:margin + length].T
        first = HALO - 32
        low_rows, high_rows = both[first:first + width], both[64 + first:64 + first + width]
        lane = lax.broadcasted_iota(jnp.int32, low_rows.shape, 1)
        return jnp.where(lane < half, low_rows, pltpu.roll(high_rows, half, 1))

    wet = own[3] > 0.0
    out_e[...] = tile(0)
    for out, flow, f in ((out_x, flow_x, 1), (out_y, flow_y, 2)):
        before = flow[...]
        out[...] = jnp.where(wet, DAMP**STEPS * before + tile(f), before)


def on_device(surface, velocity_x, velocity_y, classes, wet_mask):
    width, length = surface.shape
    wet = wet_mask.astype(jnp.float32)
    depth = (0.15 + classes.astype(jnp.float32) * (0.4 / 7.0)) * wet
    own = jnp.stack([surface, depth * velocity_x, depth * velocity_y, depth])
    rest = HALO - width
    got_1, got_2, got_3 = (move(own, "gx", steps) for steps in MOVES[:3])
    got_4 = move(own[:, :rest], "gx", MOVES[3])
    lanes = width + 2 * HALO
    f32 = jnp.float32
    packet = jax.ShapeDtypeStruct((3 * (FULL + ROW) + ROW, lanes), f32)
    centre, to_outer, to_inner, ends = pl.pallas_call(
        gather_kernel,
        out_shape=(
            jax.ShapeDtypeStruct((3, length, lanes), f32),
            packet,
            packet,
            jax.ShapeDtypeStruct((2 * ROW, lanes), f32),
        ),
        scratch_shapes=[pltpu.VMEM(packet.shape, f32)] * 2,
        compiler_params=pltpu.CompilerParams(vmem_limit_bytes=VMEM_LIMIT),
        name="turn",
    )(got_4, got_3, got_2, got_1, own)
    inner = move(to_inner, "gy", INNER)
    outer = move(to_outer, "gy", OUTER)
    total = length + 2 * HALO
    blocked = pltpu.VMEM((total // ROW, ROW, lanes), f32)
    return pl.pallas_call(
        step_kernel,
        out_shape=tuple(jax.ShapeDtypeStruct((width, length), f32) for _ in range(3)),
        scratch_shapes=[pltpu.VMEM((4, total, lanes), f32)] + [pltpu.VMEM(packet.shape, f32)] * 2 + [blocked] * 14,
        compiler_params=pltpu.CompilerParams(vmem_limit_bytes=VMEM_LIMIT),
        name="steps",
    )(outer, inner, centre, ends, own, velocity_x, velocity_y)


def solution(mesh):
    return jax.shard_map(
        on_device,
        mesh=mesh,
        in_specs=(P("gx", "gy"),) * 5,
        out_specs=(P("gx", "gy"),) * 3,
        check_vma=False,
    )
```

```python
import functools
import math

import jax
import jax.numpy as jnp
from jax import lax
from jax.experimental import pallas as pl
from jax.experimental.pallas import tpu as pltpu
from jax.sharding import PartitionSpec as P

STEPS = 8

GRAVITY = 1.0
FRICTION = 0.05
TIME_STEP = 1.2

HALO = 3 * 2 * STEPS
ROW = 8
FULL = 32
MOVE = 6
LAST = 2
VMEM_LIMIT = 8 * 1024 * 1024

R = FRICTION
POWERS = [
    (1, 0, 0, 0, 0, 0),
    (0, 1, 0, 0, 0, 0),
    (0, -R, 1, 0, 0, 0),
    (0, R**2, -R, 1, 0, 0),
    (0, -(R**3), R**2, -2 * R, 1, 0),
    (0, R**4, -(R**3), 3 * R**2, -2 * R, 1),
]
TAYLOR = [TIME_STEP**n / math.factorial(n) for n in range(5)]
E_NEXT = [sum(TAYLOR[n] * POWERS[n][i] for n in range(5)) for i in range(6)]
G_NEXT = [sum(TAYLOR[n] * POWERS[n + 1][i] for n in range(5)) for i in range(6)]
W_NEXT = [
    sum(TAYLOR[n] * (-R) ** (n - 1 - m) * POWERS[m][i] for n in range(1, 5) for m in range(n))
    for i in range(6)
]
DAMP = sum(TAYLOR[n] * (-R) ** n for n in range(5))

G_SCALE = E_NEXT[1]
K_SCALE = E_NEXT[2]
W_SCALE = W_NEXT[0]
KEPT = (1.0, G_SCALE, K_SCALE, G_SCALE * K_SCALE, K_SCALE**2, G_SCALE * K_SCALE**2)
E_MIX = E_NEXT[3] / KEPT[3]
E_MIX_2 = E_NEXT[4] / KEPT[4]
G_MIX = [G_SCALE * weight / kept for weight, kept in zip(G_NEXT, KEPT)]
W_MIX = [weight / (W_SCALE * kept) for weight, kept in zip(W_NEXT, KEPT)]


def move(cells, axis, steps):
    count = lax.axis_size(axis)
    return lax.ppermute(cells, axis, [(i, (i + steps[i % len(steps)]) % count) for i in range(count)])


MOVES = ((2, 2, -1, 1), (-1, 1, 2, 2), (1, -1), (-2,))
OUTER, INNER = (-1, 1), (1, -1)


def is_at(axis, period, *places):
    at = lax.rem(lax.axis_index(axis), period)
    return functools.reduce(jnp.logical_or, [at == place for place in places])


def turned(block, by, axis):
    return pltpu.roll(block, by % block.shape[axis], axis)


def fold(first, second):
    lane = lax.broadcasted_iota(jnp.int32, first.shape, 1)
    return jnp.where(lane < 64, pltpu.roll(first, 96, 1), pltpu.roll(second, 32, 1))


def unfold(both):
    return pltpu.roll(both, 32, 1), pltpu.roll(both, 96, 1)


def gather_kernel(got_4, got_3, got_2, got_1, own, centre, to_outer, to_inner, ends, low, high):
    rest = got_4.shape[1]
    place = [is_at("gx", 4, i) for i in range(4)]
    lower_half = is_at("gx", 4, 0, 1)

    def strip(f):
        one, two, three = got_1[f], got_2[f], got_3[f]
        return jnp.concatenate(
            [
                jnp.where(lower_half, two[-rest:], one[-rest:]),
                jnp.where(place[0], one, jnp.where(place[2], two, three)),
                own[f],
                jnp.where(place[1], one, jnp.where(place[3], two, three)),
                got_4[f],
            ],
            axis=0,
        ).T

    e, p, q, depth = (strip(f) for f in range(4))
    length = q.shape[0]
    row = lax.broadcasted_iota(jnp.int32, q.shape, 0)
    north = jnp.where(row == length - 1, 0.0, turned(q, -1, 0))
    south = jnp.where(row == 0, 0.0, turned(q, 1, 0))
    g = (-0.5 * G_SCALE) * ((turned(p, -1, 1) - turned(p, 1, 1)) + (north - south))
    ends[0:ROW], ends[ROW:] = q[:ROW], q[-ROW:]
    for f, part in enumerate((e, g, depth)):
        centre[f] = part
        at = f * (FULL + ROW)
        low[at:at + FULL] = part[:FULL]
        low[at + FULL:at + FULL + ROW] = fold(part[FULL:FULL + ROW], part[FULL + ROW:HALO])
        high[at:at + ROW] = fold(part[-HALO:ROW - HALO], part[ROW - HALO:-FULL])
        high[at + ROW:at + ROW + FULL] = part[-FULL:]
    at = 3 * (FULL + ROW)
    low[at:], high[at:] = q[:ROW], q[-ROW:]
    first_y = is_at("gy", 2, 0)
    to_inner[...] = jnp.where(first_y, high[...], low[...])
    to_outer[...] = jnp.where(first_y, low[...], high[...])


def weighted(weights, values):
    total = None
    for weight, value in zip(weights, values):
        if weight:
            term = value if weight == 1 else weight * value
            total = term if total is None else total + term
    return total


class Rows:
    def __init__(self, blocks, source):
        self.blocks, self.source, self.seam = blocks, source, {}

    def __getitem__(self, k):
        return self.source[k]

    def __setitem__(self, k, value):
        self.source[k] = value

    def over_seam(self, k):
        if k not in self.seam:
            self.seam[k] = turned(self[k], -1 if k == 0 else 1, 0)
        return self.seam[k]

    def north(self, k):
        return self[k + 1] if k < self.blocks - 1 else self.over_seam(0)

    def south(self, k):
        return self[k - 1] if k > 0 else self.over_seam(self.blocks - 1)


class Slope:
    AHEAD, LAG, SEAM = 6, 7, 1
    EDGE = ("slope_y",)

    @classmethod
    def parts(cls):
        top = 2 * cls.AHEAD
        assert 4 + 2 * cls.SEAM <= cls.LAG
        return (
            ("finish", top + 2 * cls.LAG, 2),
            ("sum_up", top, 0),
            ("slope_y", top + 2, 1),
            ("lift_y", top + 4, 2),
            ("slope_x", top + cls.LAG, 2),
            ("rotate_sum", cls.AHEAD, 0),
            ("rotate", 0, 0),
        )

    def __init__(self, blocks, ref, alpha, beta, alpha_east, beta_east, diverge=True):
        self.field = Rows(blocks, ref)
        self.alpha, self.beta, self.alpha_east, self.beta_east = alpha, beta, alpha_east, beta_east
        self.diverge = diverge
        self.east_2, self.along, self.sums_east, self.wait, self.x_west = {}, {}, {}, {}, {}
        self.dy, self.lift = {}, {}
        self.sums, self.y = Rows(blocks, {}), Rows(blocks, {})

    def rotate(self, k):
        self.east_2[k] = turned(self.field[k], -2, 1)

    def rotate_sum(self, k):
        here, east_2 = self.field[k], self.east_2.pop(k)
        self.along[k] = turned(east_2 + here, 1, 1)
        self.wait[k] = self.alpha_east[k] * (east_2 - here)

    def sum_up(self, k):
        north, south = self.field.north(k), self.field.south(k)
        self.dy[k] = north - south
        total = self.along.pop(k) + (north + south)
        self.sums[k] = total
        self.sums_east[k] = turned(total, -2, 1)

    def slope_y(self, k):
        s = self.sums
        self.y[k] = self.alpha[k] * self.dy.pop(k) + self.beta[k] * (s.north(k) - s.south(k))

    def lift_y(self, k):
        if self.diverge:
            self.lift[k] = self.y.north(k) - self.y.south(k)

    def slope_x(self, k):
        x = self.wait.pop(k) + self.beta_east[k] * (self.sums_east.pop(k) - self.sums[k])
        self.x_west[k] = turned(x, 2 if self.diverge else 1, 1)
        if self.diverge:
            self.wait[k] = x + self.lift.pop(k)

    def divergence(self, k):
        return self.wait.pop(k) - self.x_west.pop(k)


class QuickSlope:
    AHEAD, LAG, SEAM = 6, 6, 2
    EDGE = ("slope_x", "slope_y")

    @classmethod
    def parts(cls):
        assert 1 + 2 * cls.SEAM <= cls.LAG
        return (
            ("finish", cls.AHEAD + 3 + cls.LAG, 2),
            ("sum_up", cls.AHEAD, 0),
            ("slope_x", cls.AHEAD + 2, 1),
            ("slope_y", cls.AHEAD + 2, 1),
            ("lift_y", cls.AHEAD + 4, 2),
            ("rotate", 0, 0),
        )

    def __init__(self, blocks, ref, alpha, beta, alpha_east, beta_east, diverge=True):
        self.blocks, self.diverge = blocks, diverge
        self.alpha, self.beta, self.alpha_east, self.beta_east = alpha, beta, alpha_east, beta_east
        self.field = Rows(blocks, ref)
        self.at, self.far, self.dx, self.dy, self.x, self.x_west = {}, {}, {}, {}, {}, {}
        self.east_2, self.sums, self.y = (Rows(blocks, {}) for _ in range(3))

    def rotate(self, k):
        here = self.field[k]
        self.at[k] = tuple(turned(here, by, 1) for by in (-1, 1, -3))
        self.east_2[k] = turned(here, -2, 1)
        if k in (0, self.blocks - 1):
            self.field.over_seam(k)

    def sum_up(self, k):
        east_1, west_1, east_3 = self.at.pop(k)
        north, south = self.field.north(k), self.field.south(k)
        self.dy[k] = north - south
        self.sums[k] = (east_1 + west_1) + (north + south)
        self.far[k] = east_3 + east_1
        self.dx[k] = self.east_2[k] - self.field[k]
        if k in (0, self.blocks - 1):
            self.sums.over_seam(k)
            self.east_2.over_seam(k)

    def slope_x(self, k):
        sums_east = self.far.pop(k) + (self.east_2.north(k) + self.east_2.south(k))
        x = self.alpha_east[k] * self.dx.pop(k) + self.beta_east[k] * (sums_east - self.sums[k])
        self.x[k] = x
        self.x_west[k] = turned(x, 2 if self.diverge else 1, 1)

    def slope_y(self, k):
        s = self.sums
        self.y[k] = self.alpha[k] * self.dy.pop(k) + self.beta[k] * (s.north(k) - s.south(k))
        if k in (0, self.blocks - 1):
            self.y.over_seam(k)

    def lift_y(self, k):
        if self.diverge:
            self.x[k] = self.x[k] + (self.y.north(k) - self.y.south(k))

    def divergence(self, k):
        return self.x.pop(k) - self.x_west.pop(k)


class Memo:
    def __init__(self, make):
        self.make, self.made = make, {}

    def __getitem__(self, k):
        if k not in self.made:
            self.made[k] = self.make(k)
        return self.made[k]


def emit(blocks, sweeps):
    kind = type(sweeps[0][0][0])
    seam = kind.SEAM
    edge = {name: {0: seam, blocks - 1: seam} for name in kind.EDGE}
    edge["lift_y"] = {0: 2 * seam, blocks - 1: 2 * seam, 1: seam, blocks - 2: seam}
    parts = kind.parts()
    every = max(blocks, parts[0][1] + 1)
    slots = {}
    for number in range(len(sweeps)):
        for order, (name, begin, ahead) in enumerate(parts):
            for i in range(blocks):
                k = (i + ahead + 3 * number) % blocks
                slot = number * every + begin + i + edge.get(name, {}).get(k, 0)
                slots.setdefault(slot, []).append((number, order, name, k))
    for slot in sorted(slots):
        for number, _, name, k in sorted(slots[slot]):
            slopes, finish = sweeps[number]
            if name == "finish":
                finish(k)
            else:
                for slope in slopes:
                    getattr(slope, name)(k)


def step_kernel(outer, inner, centre, ends, own, flow_x, flow_y, out_e, out_x, out_y,
                rows, low, high, kept, e, g, e1, g1, total_e, *coefficients):
    length = centre.shape[1]
    total = length + 2 * HALO
    blocks = total // ROW
    first_y = is_at("gy", 2, 0)
    low[...] = jnp.where(first_y, outer[...], inner[...])
    high[...] = jnp.where(first_y, inner[...], outer[...])
    for f in range(3):
        at = f * (FULL + ROW)
        rows[f, 0:ROW], rows[f, ROW:2 * ROW] = unfold(low[at:at + ROW])
        rows[f, 2 * ROW:HALO] = low[at + ROW:at + ROW + FULL]
        rows[f, HALO:HALO + length] = centre[f]
        rows[f, HALO + length:HALO + length + FULL] = high[at:at + FULL]
        rows[f, total - 2 * ROW:total - ROW], rows[f, total - ROW:total] = unfold(high[at + FULL:at + FULL + ROW])
    last = 3 * (FULL + ROW)
    for at, given in (
        (HALO, low[last + ROW - 1:last + ROW]),
        (HALO + length - 1, -high[last:last + 1]),
        (HALO - 1, -ends[0:1]),
        (HALO + length, ends[2 * ROW - 1:2 * ROW]),
    ):
        rows[1, at:at + 1] = rows[1, at:at + 1] + (0.5 * G_SCALE) * given

    def strided(k):
        return pl.ds(k, ROW, stride=blocks)

    def set_coefficients(k, depth):
        cube = depth * depth * depth * (GRAVITY / 12.0 * K_SCALE)
        slow = 0.25 * GRAVITY * K_SCALE * depth - 4.0 * cube
        values = (slow, cube, turned(slow, -1, 1), turned(cube, -1, 1))
        for ref, value in zip(coefficients, values):
            ref[k] = value

    for k in range(blocks):
        e[k] = rows[0, strided(k), :]
        g[k] = rows[1, strided(k), :]
        set_coefficients(k, rows[2, strided(k), :])

    def weigh_in(k, parts, is_first):
        now = parts[0] + weighted(W_MIX[1:4], parts[1:4])
        total_e[k] = now if is_first else DAMP * total_e[k] + now

    def one_step(kind, count, is_first=False):
        first, second = (
            tuple(kind(count, ref, *coefficients) for ref in refs) for refs in ((e, g), (e1, g1))
        )

        def finish(k):
            e1[k], g1[k] = first[0].divergence(k), first[1].divergence(k)

        def finish_step(k):
            parts = (e[k], g[k], e1[k], g1[k], second[0].divergence(k), second[1].divergence(k))
            weigh_in(k, parts, is_first)
            e[k] = (parts[0] + parts[1]) + (parts[2] + E_MIX * parts[3]) + E_MIX_2 * parts[4]
            g[k] = weighted(G_MIX, parts)

        return [(first, finish), (second, finish_step)]

    emit(blocks, [sweep for n in range(STEPS - LAST) for sweep in one_step(Slope, blocks, n == 0)])

    margin, half = MOVE * LAST, length // 2
    few = (half + 2 * margin) // ROW
    for f, ref in ((0, e), (1, g), (3, total_e)):
        for k in range(blocks):
            rows[f, strided(k), :] = ref[k]

    def folded(f, k):
        first, second = (
            rows[f, pl.ds(HALO - margin + start + k, ROW, stride=few), :] for start in (0, half)
        )
        return fold(first, second)

    for k in range(few):
        e[k], g[k], total_e[k], kept[k] = (folded(f, k) for f in (0, 1, 3, 2))
        set_coefficients(k, kept[k])

    square = Memo(lambda k: kept[k] * kept[k] * (GRAVITY / 3.0 * W_SCALE))
    a = Memo(lambda k: -0.5 * GRAVITY * W_SCALE + 2.0 * square[k])
    b = Memo(lambda k: -0.5 * square[k])
    a_east, b_east = Memo(lambda k: turned(a[k], -1, 1)), Memo(lambda k: turned(b[k], -1, 1))
    first = tuple(QuickSlope(few, ref, *coefficients) for ref in (e, g))
    second = QuickSlope(few, e1, *coefficients)
    slope = QuickSlope(few, total_e, a, b, a_east, b_east, diverge=False)

    def finish_first(k):
        e1[k], g1[k] = first[0].divergence(k), first[1].divergence(k)
        weigh_in(k, (e[k], g[k], e1[k], g1[k]), False)

    def finish_last(k):
        at = pl.ds(k, ROW, stride=few)
        rows[0, at, :] = (e[k] + g[k]) + (e1[k] + E_MIX * g1[k]) + E_MIX_2 * second.divergence(k)
        rows[1, at, :] = slope.x_west[k]
        rows[2, at, :] = slope.y[k]

    before_last = [sweep for _ in range(LAST - 1) for sweep in one_step(QuickSlope, few)]
    emit(few, before_last + [(first, finish_first), ((second, slope), finish_last)])

    def tile(f):
        width = out_e.shape[0]
        both = rows[f, margin:margin + length].T
        first = HALO - 32
        low_rows, high_rows = both[first:first + width], both[64 + first:64 + first + width]
        lane = lax.broadcasted_iota(jnp.int32, low_rows.shape, 1)
        return jnp.where(lane < half, low_rows, pltpu.roll(high_rows, half, 1))

    wet = own[3] > 0.0
    out_e[...] = tile(0)
    for out, flow, f in ((out_x, flow_x, 1), (out_y, flow_y, 2)):
        before = flow[...]
        out[...] = jnp.where(wet, DAMP**STEPS * before + tile(f), before)


def on_device(surface, velocity_x, velocity_y, classes, wet_mask):
    width, length = surface.shape
    wet = wet_mask.astype(jnp.float32)
    depth = (0.15 + classes.astype(jnp.float32) * (0.4 / 7.0)) * wet
    own = jnp.stack([surface, depth * velocity_x, depth * velocity_y, depth])
    rest = HALO - width
    got_1, got_2, got_3 = (move(own, "gx", steps) for steps in MOVES[:3])
    got_4 = move(own[:, :rest], "gx", MOVES[3])
    lanes = width + 2 * HALO
    f32 = jnp.float32
    packet = jax.ShapeDtypeStruct((3 * (FULL + ROW) + ROW, lanes), f32)
    centre, to_outer, to_inner, ends = pl.pallas_call(
        gather_kernel,
        out_shape=(
            jax.ShapeDtypeStruct((3, length, lanes), f32),
            packet,
            packet,
            jax.ShapeDtypeStruct((2 * ROW, lanes), f32),
        ),
        scratch_shapes=[pltpu.VMEM(packet.shape, f32)] * 2,
        compiler_params=pltpu.CompilerParams(vmem_limit_bytes=VMEM_LIMIT),
        name="turn",
    )(got_4, got_3, got_2, got_1, own)
    inner = move(to_inner, "gy", INNER)
    outer = move(to_outer, "gy", OUTER)
    total = length + 2 * HALO
    blocked = pltpu.VMEM((total // ROW, ROW, lanes), f32)
    return pl.pallas_call(
        step_kernel,
        out_shape=tuple(jax.ShapeDtypeStruct((width, length), f32) for _ in range(3)),
        scratch_shapes=[pltpu.VMEM((4, total, lanes), f32)] + [pltpu.VMEM(packet.shape, f32)] * 2 + [blocked] * 10,
        compiler_params=pltpu.CompilerParams(vmem_limit_bytes=VMEM_LIMIT),
        name="steps",
    )(outer, inner, centre, ends, own, velocity_x, velocity_y)


def solution(mesh):
    return jax.shard_map(
        on_device,
        mesh=mesh,
        in_specs=(P("gx", "gy"),) * 5,
        out_specs=(P("gx", "gy"),) * 3,
        check_vma=False,
    )
```
